32 devices in a mesh: group: 2 (over y), sliver: 8 (over z, x), rep: 2 (over core).
Axes of the slice: x: 2, y: 2, z: 4, core: 2. Of those that a mesh axis runs over, the one named last changes fastest.
Arguments:
- tokens: bfloat16 [64, 4096], P(('group', 'rep', 'sliver')), parts along dimension 0, may hold values from -6 to 6
- routes: int32 [64, 2], P(('group', 'rep', 'sliver')), parts along dimension 0, may hold values from 0 to 3, all different within a row
- gate_scores: int32 [64, 2], P(('group', 'rep', 'sliver')), parts along dimension 0, may hold values from 1 to 16
- gate_weight: bfloat16 [8192, 32768], P(('group', 'sliver', 'rep')), parts along dimension 0, may hold values from -0.09375 to 0.09375
- up_weight: bfloat16 [8192, 32768], P(('group', 'sliver', 'rep')), parts along dimension 0, may hold values from -0.09375 to 0.09375
- down_weight: bfloat16 [8192, 32768], P(('group', 'sliver', 'rep')), parts along dimension 0, may hold values from -0.0625 to 0.0625
Outputs:
- mixed: bfloat16 [64, 4096], P(('group', 'rep', 'sliver')), parts along dimension 0
The draws below stay inside these ranges and needn't reach their ends.
There are 2 independent parts, one for each index of `group`. The reference program is written for one: setup_inputs(seed, part) draws one part's arguments, and reference() takes and returns one part's arrays. A program takes and returns all parts, laid end to end along the dimension named above; each array names one. Nothing has to cross between parts.
Inputs may be any that keep to these rules, and one draw needn't show every extreme that they name: `routes`: each row names 2 different experts.
All inputs are finite; a program needn't handle non-finite values.
Results may differ from the reference program's by a relative error of at most 0.0056.
Values may be sent and summed in bfloat16 or wider, within the bound.
No kernel may reach another device: no remote copies, remote signals or barrier semaphores. Data moves between devices by JAX's collectives and lax.ppermute only.
A program may use at most 448 MiB of HBM per device.

```python
import jax
import jax.numpy as jnp
from jax import lax

D = 4096
FF = 8192
EXPERTS = 4
TOPK = 2
PROBE = 32
COLS = 32768


def place_ends(result, own_key, low, top_value):
    longest = result.shape.index(max(result.shape))
    spots = []
    for shift in (0, 1):
        where = [jax.random.randint(jax.random.fold_in(own_key, axis), (), 0, length) for axis, length in enumerate(result.shape)]
        where[longest] = (where[longest] + shift) % result.shape[longest]
        spots.append(tuple(where))
    return result.at[spots[0]].set(low).at[spots[1]].set(top_value)


def levels(stream_key, dims, split, low, largest):
    loudness, own = 1.0, jax.random.fold_in(stream_key, 6)
    for dim, blocks in split:
        steps = jnp.exp(jax.random.uniform(jax.random.fold_in(own, dim), (blocks,), jnp.float32, low / len(split), largest / len(split)))
        loudness = loudness * jnp.repeat(steps, dims[dim] // blocks).reshape([-1 if axis == dim else 1 for axis in range(len(dims))])
    return loudness


def choose_distinct(own_key, rows, amount, top, lift):
    ranking = jax.random.permutation(jax.random.fold_in(own_key, 1), amount)
    pull = ranking
    for power in range(3):
        pull = pull * pull // amount
    pull = pull * lift // amount
    chance = jax.random.randint(jax.random.fold_in(own_key, 2), (rows, amount), 0, 4096) + pull
    holders = jax.random.permutation(jax.random.fold_in(own_key, 3), rows)[jnp.arange(amount) % rows]
    chance = jnp.where(jnp.arange(rows)[:, None] == holders[None, :], 1 << 14, chance)
    score = chance * amount + jnp.arange(amount)
    return lax.top_k(score.astype(jnp.int32), top)[1].astype(jnp.int32)


def centred(own_key, dims, width, limit, shards=(), kind=jnp.bfloat16):
    drawn = width * jax.random.normal(own_key, dims, jnp.float32)
    if shards:
        drawn = drawn * levels(own_key, dims, shards, -0.22, 0.18)
    return jnp.clip(drawn, -limit, limit).astype(kind)


def setup_inputs(seed: int = 0, part: int = 0) -> dict:
    seeds = jax.random.split(jax.random.key(seed), 7)
    part_keys = jax.random.split(jax.random.fold_in(seeds[6], part), 7)
    tokens = centred(part_keys[0], (PROBE, D), 1.0, 6.0, ((0, 16),))
    routes = choose_distinct(part_keys[1], PROBE, EXPERTS, TOPK, 4096)
    gate_scores = place_ends(jax.random.randint(part_keys[2], (PROBE, TOPK), 1, 17), jax.random.fold_in(part_keys[2], 1), 1, 16).astype(jnp.int32)
    gate_weight = centred(part_keys[3], (D, COLS), D ** -0.5, 0.09375, ((0, 16),))
    up_weight = centred(part_keys[4], (D, COLS), D ** -0.5, 0.09375, ((0, 16),))
    down_weight = centred(part_keys[5], (D, COLS), FF ** -0.5, 0.0625, ((0, 16),))
    return dict(tokens=tokens, routes=routes, gate_scores=gate_scores, gate_weight=gate_weight, up_weight=up_weight, down_weight=down_weight)


def combine_weights(routes, gate_scores, count):
    scores = gate_scores.astype(jnp.float32)
    share = scores / jnp.sum(scores, axis=1, keepdims=True)
    chosen = (routes[:, :, None] == jnp.arange(count, dtype=jnp.int32)[None, None, :]).astype(jnp.float32)
    return jnp.sum(share[:, :, None] * chosen, axis=1).astype(jnp.bfloat16)


def reference(tokens, routes, gate_scores, gate_weight, up_weight, down_weight):
    combine = combine_weights(routes, gate_scores, EXPERTS)
    gate = jnp.dot(tokens, gate_weight, preferred_element_type=jnp.float32)
    up = jnp.dot(tokens, up_weight, preferred_element_type=jnp.float32)
    spread = jnp.repeat(combine.astype(jnp.float32), FF, axis=1)
    hidden = (jax.nn.silu(gate) * up * spread).astype(jnp.bfloat16)
    mixed = jax.lax.dot_general(hidden, down_weight, (((1,), (1,)), ((), ())), preferred_element_type=jnp.float32)
    return mixed.astype(jnp.bfloat16)
```

```python
import functools

import jax
import jax.numpy as jnp
from jax import lax
from jax.experimental import pallas as pl
from jax.experimental.pallas import tpu as pltpu
from jax.sharding import PartitionSpec as P

EXPERTS = 4
TOPK = 2
PLANE = 4
EXTRA = 128
PARTS = 2
MIB = 1 << 20


def project_kernel(added, chunk, blocks_ref, rows_ref, *refs):
    weights = refs[: 2 * EXPERTS]
    extra = refs[2 * EXPERTS] if added else None
    out_ref, masked = refs[-2], refs[-1]
    count = rows_ref.shape[0]

    @pl.when((pl.program_id(0) == 0) & (pl.program_id(1) == 0))
    def _():
        rows = rows_ref[:, :chunk]
        for k in range(TOPK):
            route = rows_ref[:, chunk + k : chunk + k + 1].astype(jnp.float32)
            for e in range(EXPERTS):
                keep = (route == e).astype(jnp.float32).astype(jnp.bfloat16)
                masked[e, k * count : (k + 1) * count, :] = rows * keep

    slots, _, height, _ = out_ref.shape[1:]
    for g in range(2):
        total = jnp.zeros((TOPK * count, out_ref.shape[-1]), jnp.float32)
        for e in range(EXPERTS):
            total += jnp.dot(
                masked[e], weights[g * EXPERTS + e][...], preferred_element_type=jnp.float32
            )
        for t in range(slots):
            piece = total[t * height : (t + 1) * height]
            if added:
                piece += extra[0, t, g].astype(jnp.float32)
            out_ref[0, t, g] = piece.astype(out_ref.dtype)


def project(blocks, rows, gate_weight, up_weight, extra, slots, per_expert, kind):
    count, depth = rows.shape[0], gate_weight.shape[0]
    width = gate_weight.shape[1] // (EXPERTS * per_expert)
    cols = width // PARTS
    height = TOPK * count // slots
    steps = blocks.shape[0]

    def weight_spec(e):
        return pl.BlockSpec(
            (depth, cols), lambda i, j, b: (0, (e * per_expert + b[i]) * PARTS + j)
        )

    piece = pl.BlockSpec((1, slots, 2, height, cols), lambda i, j, b: (i, 0, 0, 0, j))
    whole = pl.BlockSpec(rows.shape, lambda i, j, b: (0, 0))
    specs = [whole] + [weight_spec(e) for e in range(EXPERTS)] * 2
    operands = [rows] + [gate_weight] * EXPERTS + [up_weight] * EXPERTS
    if extra is not None:
        specs.append(piece)
        operands.append(extra)
    shape = (steps, slots, 2, height, width)
    return pl.pallas_call(
        functools.partial(project_kernel, extra is not None, depth),
        out_shape=jax.ShapeDtypeStruct(shape, kind),
        grid_spec=pltpu.PrefetchScalarGridSpec(
            num_scalar_prefetch=1,
            grid=(steps, PARTS),
            in_specs=specs,
            out_specs=piece,
            scratch_shapes=[pltpu.VMEM((EXPERTS, TOPK * count, depth), jnp.bfloat16)],
        ),
        compiler_params=pltpu.CompilerParams(vmem_limit_bytes=40 * MIB),
        cost_estimate=pl.CostEstimate(
            flops=2 * TOPK * count * depth * width * 2 * EXPERTS * steps,
            bytes_accessed=2 * depth * width * 2 * EXPERTS * steps,
            transcendentals=0,
        ),
    )(blocks, *operands)


def mix_kernel(added, blocks_ref, routes_ref, *refs):
    hidden = refs[:PLANE]
    weights = refs[PLANE : PLANE + EXPERTS]
    extra = refs[PLANE + EXPERTS] if added else None
    out_ref, total = refs[-2], refs[-1]
    count = routes_ref.shape[0]
    cols = weights[0].shape[1]
    step, part = pl.program_id(0), pl.program_id(1)

    @pl.when((step == 0) & (part == 0))
    def _():
        total[...] = extra[...] if added else jnp.zeros_like(total)

    for d in range(PLANE):
        for j in range(PARTS):

            @pl.when((step == d) & (part == j))
            def _():
                block = hidden[d][:, j * cols : (j + 1) * cols]
                result = total[...]
                for e in range(EXPERTS):
                    first = (routes_ref[:, 0:1] == e).astype(jnp.float32).astype(jnp.bfloat16)
                    second = (routes_ref[:, 1:2] == e).astype(jnp.float32).astype(jnp.bfloat16)
                    chosen = block[:count] * first + block[count:] * second
                    result += lax.dot_general(
                        chosen,
                        weights[e][...],
                        (((1,), (1,)), ((), ())),
                        preferred_element_type=jnp.float32,
                    )
                total[...] = result

    @pl.when((step == PLANE - 1) & (part == PARTS - 1))
    def _():
        out_ref[...] = total[...].astype(out_ref.dtype)


def mix(blocks, routes, hidden, down_weight, extra, per_expert, kind):
    count, depth = routes.shape[0], down_weight.shape[0]
    width = down_weight.shape[1] // (EXPERTS * per_expert)
    cols = width // PARTS

    def weight_spec(e):
        return pl.BlockSpec(
            (depth, cols), lambda i, j, b: (0, (e * per_expert + b[i]) * PARTS + j)
        )

    def whole(shape):
        return pl.BlockSpec(shape, lambda i, j, b: (0, 0))

    specs = [whole(routes.shape)] + [whole(h.shape) for h in hidden]
    specs += [weight_spec(e) for e in range(EXPERTS)]
    operands = [routes, *hidden] + [down_weight] * EXPERTS
    if extra is not None:
        specs.append(whole(extra.shape))
        operands.append(extra)
    return pl.pallas_call(
        functools.partial(mix_kernel, extra is not None),
        out_shape=jax.ShapeDtypeStruct((count, depth), kind),
        grid_spec=pltpu.PrefetchScalarGridSpec(
            num_scalar_prefetch=1,
            grid=(PLANE, PARTS),
            in_specs=specs,
            out_specs=whole((count, depth)),
            scratch_shapes=[pltpu.VMEM((count, depth), jnp.float32)],
        ),
        compiler_params=pltpu.CompilerParams(vmem_limit_bytes=40 * MIB),
        cost_estimate=pl.CostEstimate(
            flops=2 * count * depth * width * EXPERTS * PLANE,
            bytes_accessed=2 * depth * width * EXPERTS * PLANE,
            transcendentals=0,
        ),
    )(blocks, *operands)


def shards(tokens, routes, gate_scores, gate_weight, up_weight, down_weight):
    slivers, cores = lax.axis_size("sliver"), lax.axis_size("rep")
    me, core = lax.axis_index("sliver"), lax.axis_index("rep")
    depth = gate_weight.shape[0]
    own_rows, model = tokens.shape
    devices = slivers * cores
    count = own_rows * devices
    slots = slivers // PLANE
    height = TOPK * count // slots
    per_expert = cores * PLANE

    def over_core(x):
        return lax.ppermute(x, "rep", [(i, i ^ 1) for i in range(cores)])

    def over_sliver(x, d):
        return lax.ppermute(x, "sliver", [(i, i ^ d) for i in range(slivers)])

    facts = jnp.concatenate([routes, gate_scores], axis=1).astype(jnp.bfloat16)
    facts = jnp.pad(facts, ((0, 0), (0, EXTRA - 2 * TOPK)))
    pieces = jnp.transpose(tokens.reshape(own_rows, slivers, cores, depth), (2, 1, 0, 3))
    pieces = pieces.reshape(devices, own_rows, depth)
    spread = jnp.broadcast_to(facts[None], (devices, own_rows, EXTRA))
    pieces = jnp.concatenate([pieces, spread], axis=2)
    rows = lax.all_to_all(pieces, ("rep", "sliver"), 0, 0, tiled=True)
    rows = rows.reshape(count, depth + EXTRA)
    facts = rows[:, depth : depth + 2 * TOPK].astype(jnp.float32)
    all_routes = facts[:, :TOPK]
    all_scores = facts[:, TOPK:]
    share = all_scores / jnp.sum(all_scores, axis=1, keepdims=True)
    share = share.astype(jnp.bfloat16).astype(jnp.float32).T.reshape(slots, height, 1)
    routes_padded = jnp.pad(all_routes, ((0, 0), (0, EXTRA - TOPK)))

    near = jnp.arange(PLANE, dtype=jnp.int32) ^ (me % PLANE)
    mine = core * PLANE + near
    theirs = (1 - core) * PLANE + near

    def projected(blocks, extra, kind):
        return project(
            blocks, rows, gate_weight, up_weight, extra, slots, per_expert, kind
        )

    sent = over_core(projected(theirs[1:], None, jnp.float32))
    sent_own = over_core(projected(theirs[:1], None, jnp.float32))
    chip = projected(mine[1:], sent, jnp.bfloat16)
    kept = projected(mine[:1], sent_own, jnp.float32)[0]
    arrived = [over_sliver(chip[d - 1], d) for d in range(1, PLANE)]
    terms = [kept] + arrived
    distance = slivers // 2
    while distance >= PLANE:
        bit = (me // distance) % 2
        length = terms[0].shape[0] // 2

        def part(which):
            total = 0.0
            for term in terms:
                piece = lax.dynamic_slice_in_dim(term, which * length, length, 0)
                total = total + piece.astype(jnp.float32)
            return total

        other = over_sliver(part(1 - bit).astype(jnp.bfloat16), distance)
        terms = [part(bit), other]
        distance //= 2
    total = sum(term.astype(jnp.float32) for term in terms)[0]
    weight = lax.dynamic_index_in_dim(share, me // PLANE, 0, keepdims=False)
    hidden = (jax.nn.silu(total[0]) * total[1] * weight).astype(jnp.bfloat16)

    distance = PLANE
    hidden = hidden[None]
    while distance < slivers:
        bit = (me // distance) % 2
        other = over_sliver(hidden, distance)
        hidden = jnp.where(
            bit == 0,
            jnp.concatenate([hidden, other], axis=0),
            jnp.concatenate([other, hidden], axis=0),
        )
        distance *= 2
    hidden = hidden.reshape(TOPK * count, hidden.shape[-1])
    own = [hidden] + [over_sliver(hidden, d) for d in range(1, PLANE)]
    others = [over_core(x) for x in own]
    partial = mix(mine, routes_padded, own, down_weight, None, per_expert, jnp.float32)
    mixed = mix(theirs, routes_padded, others, down_weight, partial, per_expert, jnp.bfloat16)

    pieces = mixed.reshape(devices, own_rows, depth)
    pieces = lax.all_to_all(pieces, ("rep", "sliver"), 0, 0, tiled=True)
    pieces = pieces.reshape(cores, slivers, own_rows, depth)
    return jnp.transpose(pieces, (2, 1, 0, 3)).reshape(own_rows, model)


def solution(mesh):
    return jax.shard_map(
        shards,
        mesh=mesh,
        in_specs=(
            P(("group", "rep", "sliver"), None),
            P(("group", "rep", "sliver"), None),
            P(("group", "rep", "sliver"), None),
            P(("group", "sliver", "rep"), None),
            P(("group", "sliver", "rep"), None),
            P(("group", "sliver", "rep"), None),
        ),
        out_specs=P(("group", "rep", "sliver"), None),
        check_vma=False,
    )
```

```python
import functools

import jax
import jax.numpy as jnp
from jax import lax
from jax.experimental import pallas as pl
from jax.experimental.pallas import tpu as pltpu
from jax.sharding import PartitionSpec as P

EXPERTS = 4
TOPK = 2
PLANE = 4
EXTRA = 128
CHUNKS = 1
MIB = 1 << 20
ANY = pl.BlockSpec(memory_space=pl.ANY)
VMEM = pl.BlockSpec(memory_space=pltpu.VMEM)
SMEM = pl.BlockSpec(memory_space=pltpu.SMEM)


def in_hbm(x):
    return pltpu.with_memory_space_constraint(x, pltpu.HBM)


def limit(*sizes):
    return pltpu.CompilerParams(vmem_limit_bytes=min(sum(sizes) + 6 * MIB, 60 * MIB))


def pack_kernel(tokens_ref, routes_ref, scores_ref, out_ref):
    devices, own_rows, width = out_ref.shape
    depth = width - EXTRA
    cores = 2
    slivers = devices // cores
    lane = lax.broadcasted_iota(jnp.int32, (own_rows, EXTRA), 1)
    facts = jnp.zeros((own_rows, EXTRA), jnp.int32)
    for k in range(TOPK):
        facts = jnp.where(lane == k, routes_ref[:, k : k + 1], facts)
        facts = jnp.where(lane == TOPK + k, scores_ref[:, k : k + 1], facts)
    facts = facts.astype(jnp.float32).astype(out_ref.dtype)
    for r in range(cores):
        for s in range(slivers):
            first = (s * cores + r) * depth
            out_ref[r * slivers + s, :, :depth] = tokens_ref[:, first : first + depth]
            out_ref[r * slivers + s, :, depth:] = facts


def packed(tokens, routes, gate_scores, slivers, cores, depth):
    own_rows = tokens.shape[0]
    devices = slivers * cores
    if depth % 128 == 0 and cores == 2:
        return pl.pallas_call(
            pack_kernel,
            out_shape=jax.ShapeDtypeStruct((devices, own_rows, depth + EXTRA), tokens.dtype),
            in_specs=[VMEM] * 3,
            out_specs=VMEM,
        )(tokens, routes, gate_scores)
    facts = jnp.concatenate([routes, gate_scores], axis=1).astype(tokens.dtype)
    facts = jnp.pad(facts, ((0, 0), (0, EXTRA - 2 * TOPK)))
    pieces = jnp.transpose(tokens.reshape(own_rows, slivers, cores, depth), (2, 1, 0, 3))
    pieces = pieces.reshape(devices, own_rows, depth)
    spread = jnp.broadcast_to(facts[None], (devices, own_rows, EXTRA))
    return jnp.concatenate([pieces, spread], axis=2)


def after(x, *before):
    return lax.optimization_barrier((x, *before))[0]


def project_kernel(blocks_ref, rows_ref, gate_ref, up_ref, *refs):
    outs, (masked, buffer, sems) = refs[:-3], refs[-3:]
    places = [(out, i) for out in outs for i in range(out.shape[0])]
    steps = len(places)
    _, slots, _, height, cols = outs[0].shape
    depth = gate_ref.shape[0]
    count = rows_ref.shape[0]
    per_expert = gate_ref.shape[1] // (EXPERTS * cols)
    copies = []
    for i in range(steps):
        for g, ref in enumerate((gate_ref, up_ref)):
            for e in range(EXPERTS):
                first = pl.multiple_of((e * per_expert + blocks_ref[i]) * cols, cols)
                copies.append(
                    pltpu.make_async_copy(
                        ref.at[:, pl.ds(first, cols)],
                        buffer.at[i, g, pl.ds(e * depth, depth)],
                        sems.at[i, g, e],
                    )
                )
                copies[-1].start()
    rows = rows_ref[:, :depth]
    for k in range(TOPK):
        route = rows_ref[:, depth + k : depth + k + 1].astype(jnp.float32)
        for e in range(EXPERTS):
            keep = (route == e).astype(jnp.float32).astype(jnp.bfloat16)
            masked[k * count : (k + 1) * count, e * depth : (e + 1) * depth] = rows * keep
    for i in range(steps):
        for g in range(2):
            for e in range(EXPERTS):
                copies[(i * 2 + g) * EXPERTS + e].wait()
            total = jnp.dot(masked[...], buffer[i, g], preferred_element_type=jnp.float32)
            out, at = places[i]
            out[at, :, g] = total.reshape(slots, height, cols).astype(out.dtype)


def project(blocks, splits, kinds, rows, gate_weight, up_weight, slots, width):
    depth = gate_weight.shape[0]
    pairs = TOPK * rows.shape[0]
    steps = sum(splits)
    shapes = [(n, slots, 2, pairs // slots, width) for n in splits]
    weights = steps * 2 * EXPERTS * depth * width
    return pl.pallas_call(
        project_kernel,
        out_shape=[jax.ShapeDtypeStruct(s, k) for s, k in zip(shapes, kinds)],
        in_specs=[SMEM, VMEM, ANY, ANY],
        out_specs=[VMEM] * len(splits),
        scratch_shapes=[
            pltpu.VMEM((pairs, EXPERTS * depth), jnp.bfloat16),
            pltpu.VMEM((steps, 2, EXPERTS * depth, width), jnp.bfloat16),
            pltpu.SemaphoreType.DMA((steps, 2, EXPERTS)),
        ],
        compiler_params=limit(2 * weights, 8 * steps * pairs * width),
        cost_estimate=pl.CostEstimate(
            flops=2 * pairs * weights, bytes_accessed=2 * weights, transcendentals=0
        ),
    )(blocks, rows, in_hbm(gate_weight), in_hbm(up_weight))


def mix_kernel(steps, added, blocks_ref, routes_ref, *refs):
    hidden, refs = refs[:steps], refs[steps:]
    down_ref, refs = refs[0], refs[1:]
    extra = refs[0] if added else None
    out_ref, stacked, buffer, sems = refs[-4:]
    count, depth = out_ref.shape
    cols = hidden[0].shape[1]
    per_expert = down_ref.shape[1] // (EXPERTS * cols)
    copies = []
    for i in range(steps):
        for e in range(EXPERTS):
            first = pl.multiple_of((e * per_expert + blocks_ref[i]) * cols, cols)
            copies.append(
                pltpu.make_async_copy(
                    down_ref.at[:, pl.ds(first, cols)],
                    buffer.at[i, e],
                    sems.at[i, e],
                )
            )
            copies[-1].start()
    masks = [
        [(routes_ref[:, k : k + 1] == e).astype(jnp.float32) for k in range(TOPK)]
        for e in range(EXPERTS)
    ]
    for e in range(EXPERTS):
        keep = [jnp.broadcast_to(m, (count, cols)).astype(jnp.bfloat16) for m in masks[e]]
        for i in range(steps):
            stacked[i, e] = sum(hidden[i][k * count : (k + 1) * count] * keep[k] for k in range(TOPK))

    def step(i, total):
        for e in range(EXPERTS):
            pltpu.make_async_copy(buffer.at[i, e], buffer.at[i, e], sems.at[i, e]).wait()
        for e in range(EXPERTS):
            total += lax.dot_general(
                stacked[i, e],
                buffer[i, e],
                (((1,), (1,)), ((), ())),
                preferred_element_type=jnp.float32,
            )
        return total

    total = extra[...] if added else jnp.zeros((count, depth), jnp.float32)
    total = lax.fori_loop(0, steps, step, total)
    out_ref[...] = total.astype(out_ref.dtype)


def mix(blocks, routes, hidden, down_weight, extra, kind):
    count, depth = routes.shape[0], down_weight.shape[0]
    width = hidden[0].shape[1]
    steps = len(hidden)
    room = 16 * steps * count * width
    if room > 32 * MIB and steps > 1:
        part = steps // 2
        extra = mix(blocks[:part], routes, hidden[:part], down_weight, extra, jnp.float32)
        return mix(blocks[part:], routes, hidden[part:], down_weight, extra, kind)
    weights = steps * EXPERTS * depth * width
    operands = [blocks, routes, *hidden, in_hbm(down_weight)]
    specs = [SMEM] + [VMEM] * (1 + steps) + [ANY]
    if extra is not None:
        operands.append(extra)
        specs.append(VMEM)
    return pl.pallas_call(
        functools.partial(mix_kernel, steps, extra is not None),
        out_shape=jax.ShapeDtypeStruct((count, depth), kind),
        in_specs=specs,
        out_specs=VMEM,
        scratch_shapes=[
            pltpu.VMEM((steps, EXPERTS, count, width), jnp.bfloat16),
            pltpu.VMEM((steps, EXPERTS, depth, width), jnp.bfloat16),
            pltpu.SemaphoreType.DMA((steps, EXPERTS)),
        ],
        compiler_params=limit(2 * weights, room),
        cost_estimate=pl.CostEstimate(
            flops=2 * count * weights, bytes_accessed=2 * weights, transcendentals=0
        ),
    )(*operands)


def shards(tokens, routes, gate_scores, gate_weight, up_weight, down_weight):
    slivers, cores = lax.axis_size("sliver"), lax.axis_size("rep")
    me, core = lax.axis_index("sliver"), lax.axis_index("rep")
    depth, columns = gate_weight.shape
    own_rows, model = tokens.shape
    devices = slivers * cores
    count = own_rows * devices
    slots = slivers // PLANE
    height = TOPK * count // slots
    width = columns // (EXPERTS * cores * PLANE * CHUNKS)

    def over_core(x):
        return lax.ppermute(x, "rep", [(i, i ^ 1) for i in range(cores)])

    def over_sliver(x, d):
        return lax.ppermute(x, "sliver", [(i, i ^ d) for i in range(slivers)])

    pieces = packed(tokens, routes, gate_scores, slivers, cores, depth)
    rows = lax.all_to_all(pieces, ("rep", "sliver"), 0, 0, tiled=True)
    rows = rows.reshape(count, depth + EXTRA)
    facts = rows[:, depth : depth + 2 * TOPK].astype(jnp.float32)
    all_routes = facts[:, :TOPK]
    all_scores = facts[:, TOPK:]
    share = all_scores / jnp.sum(all_scores, axis=1, keepdims=True)
    share = share.astype(jnp.bfloat16).astype(jnp.float32).T.reshape(slots, height, 1)
    weight = lax.dynamic_index_in_dim(share, me // PLANE, 0, keepdims=False)
    routes_padded = jnp.pad(all_routes, ((0, 0), (0, EXTRA - TOPK)))

    near = jnp.arange(PLANE, dtype=jnp.int32) ^ (me % PLANE)
    mine = (core * PLANE + near) * CHUNKS
    theirs = ((1 - core) * PLANE + near) * CHUNKS

    def projected(blocks, splits, kinds=(jnp.float32,)):
        return project(blocks, splits, kinds, rows, gate_weight, up_weight, slots, width)

    far, far_own = projected(
        jnp.concatenate([theirs[1:], theirs[:1]]), (PLANE - 1, 1), (jnp.float32, jnp.bfloat16)
    )
    far, far_own = over_core(far), over_core(far_own)
    (chip,) = projected(mine[1:], (PLANE - 1,))
    chip = (chip + far).astype(jnp.bfloat16)
    (kept,) = projected(after(mine[:1], chip), (1,))
    halves = 2 if slots > 1 else 1
    top = me // (slivers // 2) if halves == 2 else 0
    length = slots // halves

    def half(x, which):
        return lax.dynamic_slice_in_dim(x, which * length, length, 0)

    terms = []
    for which in [1 - top, top][2 - halves :]:
        sent = [half(chip[d - 1], which) for d in range(1, PLANE)]
        arrived = [over_sliver(sent[d - 1], d) for d in range(1, PLANE)]
        terms.append(arrived + [half(kept[0], which), half(far_own[0], which)])

    def summed(terms):
        return sum(term.astype(jnp.float32) for term in terms)

    gathered = []
    for c in range(CHUNKS):
        distance = slivers // 2
        parts = terms[-1]
        if halves == 2:
            parts = parts + [over_sliver(summed(terms[0]).astype(jnp.bfloat16), distance)]
            distance //= 2
        while distance >= PLANE:
            bit = (me // distance) % 2
            length = parts[0].shape[0] // 2

            def part(which):
                return summed(
                    [lax.dynamic_slice_in_dim(x, which * length, length, 0) for x in parts]
                )

            other = over_sliver(part(1 - bit).astype(jnp.bfloat16), distance)
            parts = [part(bit), other]
            distance //= 2
        total = sum(term.astype(jnp.float32) for term in parts)[0]
        hidden = (jax.nn.silu(total[0]) * total[1] * weight).astype(jnp.bfloat16)[None]
        distance = PLANE
        while distance < slivers:
            bit = (me // distance) % 2
            other = over_sliver(hidden, distance)
            hidden = jnp.where(
                bit == 0,
                jnp.concatenate([hidden, other], axis=0),
                jnp.concatenate([other, hidden], axis=0),
            )
            distance *= 2
        hidden = hidden.reshape(TOPK * count, width)
        gathered.append([hidden] + [over_sliver(hidden, d) for d in range(1, PLANE)])

    (gathered,) = gathered
    order = jnp.stack([mine[0], theirs[0]])
    first = [gathered[0], over_core(gathered[0])]
    mixed = mix(order, routes_padded, first, down_weight, None, jnp.float32)
    rest = [after(x, mixed) for x in gathered[1:]]
    rest_other = [over_core(x) for x in rest]
    order = jnp.concatenate([mine[1:], theirs[1:]])
    mixed = mix(order, routes_padded, rest + rest_other, down_weight, mixed, jnp.bfloat16)

    pieces = mixed.reshape(devices, own_rows, depth)
    pieces = lax.all_to_all(pieces, ("rep", "sliver"), 0, 0, tiled=True)
    pieces = pieces.reshape(cores, slivers, own_rows, depth)
    return jnp.transpose(pieces, (2, 1, 0, 3)).reshape(own_rows, model)


def solution(mesh):
    return jax.shard_map(
        shards,
        mesh=mesh,
        in_specs=(
            P(("group", "rep", "sliver"), None),
            P(("group", "rep", "sliver"), None),
            P(("group", "rep", "sliver"), None),
            P(("group", "sliver", "rep"), None),
            P(("group", "sliver", "rep"), None),
            P(("group", "sliver", "rep"), None),
        ),
        out_specs=P(("group", "rep", "sliver"), None),
        check_vma=False,
    )
```

```python
import functools

import jax
import jax.numpy as jnp
from jax import lax
from jax.experimental import pallas as pl
from jax.experimental.pallas import tpu as pltpu
from jax.sharding import PartitionSpec as P

EXPERTS = 4
TOPK = 2
PLANE = 4
EXTRA = 128
CHUNKS = 1
MIB = 1 << 20
ANY = pl.BlockSpec(memory_space=pl.ANY)
VMEM = pl.BlockSpec(memory_space=pltpu.VMEM)


def in_hbm(x):
    return pltpu.with_memory_space_constraint(x, pltpu.HBM)


def limit(*sizes):
    return pltpu.CompilerParams(vmem_limit_bytes=min(sum(sizes) + 6 * MIB, 60 * MIB))


def pack_kernel(tokens_hbm, routes_hbm, scores_hbm, out_ref, *scratch):
    tokens_ref, routes_ref, scores_ref, sems = scratch
    copies = [
        pltpu.make_async_copy(source, target, sems.at[i])
        for i, (source, target) in enumerate(zip((tokens_hbm, routes_hbm, scores_hbm), scratch))
    ]
    for copy in copies:
        copy.start()
    for copy in copies:
        copy.wait()
    devices, own_rows, width = out_ref.shape
    depth = width - EXTRA
    cores = 2
    slivers = devices // cores
    lane = lax.broadcasted_iota(jnp.int32, (own_rows, EXTRA), 1)
    facts = jnp.zeros((own_rows, EXTRA), jnp.int32)
    for k in range(TOPK):
        facts = jnp.where(lane == k, routes_ref[:, k : k + 1], facts)
        facts = jnp.where(lane == TOPK + k, scores_ref[:, k : k + 1], facts)
    facts = facts.astype(jnp.float32).astype(out_ref.dtype)
    for r in range(cores):
        for s in range(slivers):
            first = (s * cores + r) * depth
            out_ref[r * slivers + s, :, :depth] = tokens_ref[:, first : first + depth]
            out_ref[r * slivers + s, :, depth:] = facts


def packed(tokens, routes, gate_scores, slivers, cores, depth):
    own_rows = tokens.shape[0]
    devices = slivers * cores
    if depth % 128 == 0 and cores == 2:
        return pl.pallas_call(
            pack_kernel,
            out_shape=pltpu.MemorySpace.VMEM((devices, own_rows, depth + EXTRA), tokens.dtype),
            in_specs=[ANY] * 3,
            out_specs=VMEM,
            scratch_shapes=[
                *[pltpu.VMEM(x.shape, x.dtype) for x in (tokens, routes, gate_scores)],
                pltpu.SemaphoreType.DMA((3,)),
            ],
        )(in_hbm(tokens), in_hbm(routes), in_hbm(gate_scores))
    facts = jnp.concatenate([routes, gate_scores], axis=1).astype(tokens.dtype)
    facts = jnp.pad(facts, ((0, 0), (0, EXTRA - 2 * TOPK)))
    pieces = jnp.transpose(tokens.reshape(own_rows, slivers, cores, depth), (2, 1, 0, 3))
    pieces = pieces.reshape(devices, own_rows, depth)
    spread = jnp.broadcast_to(facts[None], (devices, own_rows, EXTRA))
    return jnp.concatenate([pieces, spread], axis=2)


def after(x, *before):
    return lax.optimization_barrier((x, *before))[0]


def own_block(d):
    return lax.axis_index("rep") * PLANE + lax.bitwise_xor(lax.axis_index("sliver") % PLANE, d)


def other_block(d):
    return PLANE - lax.axis_index("rep") * PLANE + lax.bitwise_xor(
        lax.axis_index("sliver") % PLANE, d
    )


def project_kernel(blocks, rows_ref, gate_ref, up_ref, *refs):
    outs, (masked, buffer, sems) = refs[:-3], refs[-3:]
    places = [(out, i) for out in outs for i in range(out.shape[0])]
    steps = len(places)
    _, slots, _, height, cols = outs[0].shape
    depth = gate_ref.shape[0]
    count = rows_ref.shape[0]
    per_expert = gate_ref.shape[1] // (EXPERTS * cols)
    copies = []
    for i, (where, d) in enumerate(blocks):
        block = where(d)
        for g, ref in enumerate((gate_ref, up_ref)):
            for e in range(EXPERTS):
                first = pl.multiple_of((e * per_expert + block) * cols, cols)
                copies.append(
                    pltpu.make_async_copy(
                        ref.at[:, pl.ds(first, cols)],
                        buffer.at[i, g, pl.ds(e * depth, depth)],
                        sems.at[i, g, e],
                    )
                )
                copies[-1].start()
    rows = rows_ref[:, :depth]
    for k in range(TOPK):
        route = rows_ref[:, depth + k : depth + k + 1].astype(jnp.float32)
        for e in range(EXPERTS):
            keep = (route == e).astype(jnp.float32).astype(jnp.bfloat16)
            masked[k * count : (k + 1) * count, e * depth : (e + 1) * depth] = rows * keep
    for i in range(steps):
        for g in range(2):
            for e in range(EXPERTS):
                copies[(i * 2 + g) * EXPERTS + e].wait()
            total = jnp.dot(masked[...], buffer[i, g], preferred_element_type=jnp.float32)
            out, at = places[i]
            out[at, :, g] = total.reshape(slots, height, cols).astype(out.dtype)


def project(blocks, splits, kinds, rows, gate_weight, up_weight, slots, width):
    depth = gate_weight.shape[0]
    pairs = TOPK * rows.shape[0]
    steps = sum(splits)
    shapes = [(n, slots, 2, pairs // slots, width) for n in splits]
    weights = steps * 2 * EXPERTS * depth * width
    return pl.pallas_call(
        functools.partial(project_kernel, blocks),
        out_shape=[jax.ShapeDtypeStruct(s, k) for s, k in zip(shapes, kinds)],
        in_specs=[VMEM, ANY, ANY],
        out_specs=[VMEM] * len(splits),
        scratch_shapes=[
            pltpu.VMEM((pairs, EXPERTS * depth), jnp.bfloat16),
            pltpu.VMEM((steps, 2, EXPERTS * depth, width), jnp.bfloat16),
            pltpu.SemaphoreType.DMA((steps, 2, EXPERTS)),
        ],
        compiler_params=limit(2 * weights, 8 * steps * pairs * width),
        cost_estimate=pl.CostEstimate(
            flops=2 * pairs * weights, bytes_accessed=2 * weights, transcendentals=0
        ),
    )(rows, in_hbm(gate_weight), in_hbm(up_weight))


def mix_kernel(blocks, added, routes_ref, *refs):
    steps = len(blocks)
    hidden, refs = refs[:steps], refs[steps:]
    down_ref, refs = refs[0], refs[1:]
    extra = refs[0] if added else None
    out_ref, stacked, buffer, sems = refs[-4:]
    count, depth = out_ref.shape
    cols = hidden[0].shape[1]
    per_expert = down_ref.shape[1] // (EXPERTS * cols)
    copies = []
    for i, (where, d) in enumerate(blocks):
        block = where(d)
        for e in range(EXPERTS):
            first = pl.multiple_of((e * per_expert + block) * cols, cols)
            copies.append(
                pltpu.make_async_copy(
                    down_ref.at[:, pl.ds(first, cols)],
                    buffer.at[i, e],
                    sems.at[i, e],
                )
            )
            copies[-1].start()
    masks = [
        [(routes_ref[:, k : k + 1] == e).astype(jnp.float32) for k in range(TOPK)]
        for e in range(EXPERTS)
    ]
    for e in range(EXPERTS):
        keep = [jnp.broadcast_to(m, (count, cols)).astype(jnp.bfloat16) for m in masks[e]]
        for i in range(steps):
            stacked[i, e] = sum(hidden[i][k * count : (k + 1) * count] * keep[k] for k in range(TOPK))

    def step(i, total):
        for e in range(EXPERTS):
            pltpu.make_async_copy(buffer.at[i, e], buffer.at[i, e], sems.at[i, e]).wait()
        for e in range(EXPERTS):
            total += lax.dot_general(
                stacked[i, e],
                buffer[i, e],
                (((1,), (1,)), ((), ())),
                preferred_element_type=jnp.float32,
            )
        return total

    total = extra[...] if added else jnp.zeros((count, depth), jnp.float32)
    total = lax.fori_loop(0, steps, step, total)
    out_ref[...] = total.astype(out_ref.dtype)


def mix(blocks, routes, hidden, down_weight, extra, kind):
    count, depth = routes.shape[0], down_weight.shape[0]
    width = hidden[0].shape[1]
    steps = len(hidden)
    room = 16 * steps * count * width
    if room > 32 * MIB and steps > 1:
        part = steps // 2
        extra = mix(blocks[:part], routes, hidden[:part], down_weight, extra, jnp.float32)
        return mix(blocks[part:], routes, hidden[part:], down_weight, extra, kind)
    weights = steps * EXPERTS * depth * width
    operands = [routes, *hidden, in_hbm(down_weight)]
    specs = [VMEM] * (1 + steps) + [ANY]
    if extra is not None:
        operands.append(extra)
        specs.append(VMEM)
    return pl.pallas_call(
        functools.partial(mix_kernel, blocks, extra is not None),
        out_shape=jax.ShapeDtypeStruct((count, depth), kind),
        in_specs=specs,
        out_specs=VMEM,
        scratch_shapes=[
            pltpu.VMEM((steps, EXPERTS, count, width), jnp.bfloat16),
            pltpu.VMEM((steps, EXPERTS, depth, width), jnp.bfloat16),
            pltpu.SemaphoreType.DMA((steps, EXPERTS)),
        ],
        compiler_params=limit(2 * weights, room),
        cost_estimate=pl.CostEstimate(
            flops=2 * count * weights, bytes_accessed=2 * weights, transcendentals=0
        ),
    )(*operands)


def shards(tokens, routes, gate_scores, gate_weight, up_weight, down_weight):
    slivers, cores = lax.axis_size("sliver"), lax.axis_size("rep")
    me, core = lax.axis_index("sliver"), lax.axis_index("rep")
    depth, columns = gate_weight.shape
    own_rows, model = tokens.shape
    devices = slivers * cores
    count = own_rows * devices
    slots = slivers // PLANE
    height = TOPK * count // slots
    width = columns // (EXPERTS * cores * PLANE * CHUNKS)

    def over_core(x):
        return lax.ppermute(x, "rep", [(i, i ^ 1) for i in range(cores)])

    def over_sliver(x, d):
        return lax.ppermute(x, "sliver", [(i, i ^ d) for i in range(slivers)])

    pieces = packed(tokens, routes, gate_scores, slivers, cores, depth)
    rows = lax.all_to_all(pieces, ("rep", "sliver"), 0, 0, tiled=True)
    rows = rows.reshape(count, depth + EXTRA)
    facts = rows[:, depth : depth + 2 * TOPK].astype(jnp.float32)
    all_routes = facts[:, :TOPK]
    all_scores = facts[:, TOPK:]
    share = all_scores / jnp.sum(all_scores, axis=1, keepdims=True)
    share = share.astype(jnp.bfloat16).astype(jnp.float32).T.reshape(slots, height, 1)
    weight = lax.dynamic_index_in_dim(share, me // PLANE, 0, keepdims=False)
    routes_padded = jnp.pad(all_routes, ((0, 0), (0, EXTRA - TOPK)))

    mine = [(own_block, d) for d in range(PLANE)]
    theirs = [(other_block, d) for d in range(PLANE)]

    def projected(blocks, splits, kinds=(jnp.float32,), before=None):
        given = rows if before is None else after(rows, before)
        return project(blocks, splits, kinds, given, gate_weight, up_weight, slots, width)

    far, far_own = projected(
        theirs[1:] + theirs[:1], (PLANE - 1, 1), (jnp.float32, jnp.bfloat16)
    )
    far, far_own = over_core(far), over_core(far_own)
    (chip,) = projected(mine[1:], (PLANE - 1,))
    chip = (chip + far).astype(jnp.bfloat16)
    (kept,) = projected(mine[:1], (1,), before=chip)
    halves = 2 if slots > 1 else 1
    top = me // (slivers // 2) if halves == 2 else 0
    length = slots // halves

    def half(x, which):
        return lax.dynamic_slice_in_dim(x, which * length, length, 0)

    terms = []
    for which in [1 - top, top][2 - halves :]:
        sent = [half(chip[d - 1], which) for d in range(1, PLANE)]
        arrived = [over_sliver(sent[d - 1], d) for d in range(1, PLANE)]
        terms.append(arrived + [half(kept[0], which), half(far_own[0], which)])

    def summed(terms):
        return sum(term.astype(jnp.float32) for term in terms)

    gathered = []
    for c in range(CHUNKS):
        distance = slivers // 2
        parts = terms[-1]
        if halves == 2:
            parts = parts + [over_sliver(summed(terms[0]).astype(jnp.bfloat16), distance)]
            distance //= 2
        while distance >= PLANE:
            bit = (me // distance) % 2
            length = parts[0].shape[0] // 2

            def part(which):
                return summed(
                    [lax.dynamic_slice_in_dim(x, which * length, length, 0) for x in parts]
                )

            other = over_sliver(part(1 - bit).astype(jnp.bfloat16), distance)
            parts = [part(bit), other]
            distance //= 2
        total = sum(term.astype(jnp.float32) for term in parts)[0]
        hidden = (jax.nn.silu(total[0]) * total[1] * weight).astype(jnp.bfloat16)[None]
        distance = PLANE
        while distance < slivers:
            bit = (me // distance) % 2
            other = over_sliver(hidden, distance)
            hidden = jnp.where(
                bit == 0,
                jnp.concatenate([hidden, other], axis=0),
                jnp.concatenate([other, hidden], axis=0),
            )
            distance *= 2
        hidden = hidden.reshape(TOPK * count, width)
        gathered.append([hidden] + [over_sliver(hidden, d) for d in range(1, PLANE)])

    (gathered,) = gathered
    order = mine[:1] + theirs[:1]
    first = [gathered[0], over_core(gathered[0])]
    mixed = mix(order, routes_padded, first, down_weight, None, jnp.float32)
    rest = [after(x, mixed) for x in gathered[1:]]
    rest_other = [over_core(x) for x in rest]
    order = mine[1:] + theirs[1:]
    mixed = mix(order, routes_padded, rest + rest_other, down_weight, mixed, jnp.bfloat16)

    pieces = mixed.reshape(devices, own_rows, depth)
    pieces = lax.all_to_all(pieces, ("rep", "sliver"), 0, 0, tiled=True)
    pieces = pieces.reshape(cores, slivers, own_rows, depth)
    return jnp.transpose(pieces, (2, 1, 0, 3)).reshape(own_rows, model)


def solution(mesh):
    return jax.shard_map(
        shards,
        mesh=mesh,
        in_specs=(
            P(("group", "rep", "sliver"), None),
            P(("group", "rep", "sliver"), None),
            P(("group", "rep", "sliver"), None),
            P(("group", "sliver", "rep"), None),
            P(("group", "sliver", "rep"), None),
            P(("group", "sliver", "rep"), None),
        ),
        out_specs=P(("group", "rep", "sliver"), None),
        check_vma=False,
    )
```

```python
import functools

import jax
import jax.numpy as jnp
from jax import lax
from jax.experimental import pallas as pl
from jax.experimental.pallas import tpu as pltpu
from jax.sharding import PartitionSpec as P

EXPERTS = 4
TOPK = 2
PLANE = 4
EXTRA = 128
CHUNKS = 1
MIB = 1 << 20
ANY = pl.BlockSpec(memory_space=pl.ANY)
VMEM = pl.BlockSpec(memory_space=pltpu.VMEM)


def in_hbm(x):
    return pltpu.with_memory_space_constraint(x, pltpu.HBM)


def limit(*sizes):
    return pltpu.CompilerParams(vmem_limit_bytes=min(sum(sizes) + 6 * MIB, 60 * MIB))


def pack_kernel(tokens_hbm, routes_hbm, scores_hbm, out_ref, *scratch):
    tokens_ref, routes_ref, scores_ref, sems = scratch
    copies = [
        pltpu.make_async_copy(source, target, sems.at[i])
        for i, (source, target) in enumerate(zip((tokens_hbm, routes_hbm, scores_hbm), scratch))
    ]
    for copy in copies:
        copy.start()
    for copy in copies:
        copy.wait()
    devices, own_rows, width = out_ref.shape
    depth = width - EXTRA
    cores = 2
    slivers = devices // cores
    lane = lax.broadcasted_iota(jnp.int32, (own_rows, EXTRA), 1)
    facts = jnp.zeros((own_rows, EXTRA), jnp.int32)
    for k in range(TOPK):
        facts = jnp.where(lane == k, routes_ref[:, k : k + 1], facts)
        facts = jnp.where(lane == TOPK + k, scores_ref[:, k : k + 1], facts)
    facts = facts.astype(jnp.float32).astype(out_ref.dtype)
    for r in range(cores):
        for s in range(slivers):
            first = (s * cores + r) * depth
            out_ref[r * slivers + s, :, :depth] = tokens_ref[:, first : first + depth]
            out_ref[r * slivers + s, :, depth:] = facts


def packed(tokens, routes, gate_scores, slivers, cores, depth):
    own_rows = tokens.shape[0]
    devices = slivers * cores
    if depth % 128 == 0 and cores == 2:
        return pl.pallas_call(
            pack_kernel,
            out_shape=pltpu.MemorySpace.VMEM((devices, own_rows, depth + EXTRA), tokens.dtype),
            in_specs=[ANY] * 3,
            out_specs=VMEM,
            scratch_shapes=[
                *[pltpu.VMEM(x.shape, x.dtype) for x in (tokens, routes, gate_scores)],
                pltpu.SemaphoreType.DMA((3,)),
            ],
        )(in_hbm(tokens), in_hbm(routes), in_hbm(gate_scores))
    facts = jnp.concatenate([routes, gate_scores], axis=1).astype(tokens.dtype)
    facts = jnp.pad(facts, ((0, 0), (0, EXTRA - 2 * TOPK)))
    pieces = jnp.transpose(tokens.reshape(own_rows, slivers, cores, depth), (2, 1, 0, 3))
    pieces = pieces.reshape(devices, own_rows, depth)
    spread = jnp.broadcast_to(facts[None], (devices, own_rows, EXTRA))
    return jnp.concatenate([pieces, spread], axis=2)


def after(x, *before):
    return lax.optimization_barrier((x, *before))[0]


def own_block(d):
    return lax.axis_index("rep") * PLANE + lax.bitwise_xor(lax.axis_index("sliver") % PLANE, d)


def other_block(d):
    return PLANE - lax.axis_index("rep") * PLANE + lax.bitwise_xor(
        lax.axis_index("sliver") % PLANE, d
    )


def project_kernel(blocks, rows_ref, gate_ref, up_ref, *refs):
    outs, (masked, buffer, sems) = refs[:-3], refs[-3:]
    places = [(out, i) for out in outs for i in range(out.shape[0])]
    steps = len(places)
    _, slots, _, height, cols = outs[0].shape
    depth = gate_ref.shape[0]
    count = rows_ref.shape[0]
    per_expert = gate_ref.shape[1] // (EXPERTS * cols)
    copies = []
    for i, (where, d) in enumerate(blocks):
        block = where(d)
        for g, ref in enumerate((gate_ref, up_ref)):
            for e in range(EXPERTS):
                first = pl.multiple_of((e * per_expert + block) * cols, cols)
                copies.append(
                    pltpu.make_async_copy(
                        ref.at[:, pl.ds(first, cols)],
                        buffer.at[i, g, pl.ds(e * depth, depth)],
                        sems.at[i, g, e],
                    )
                )
                copies[-1].start()
    rows = rows_ref[:, :depth]
    for k in range(TOPK):
        route = rows_ref[:, depth + k : depth + k + 1].astype(jnp.float32)
        for e in range(EXPERTS):
            keep = (route == e).astype(jnp.float32).astype(jnp.bfloat16)
            masked[k * count : (k + 1) * count, e * depth : (e + 1) * depth] = rows * keep
    for i in range(steps):
        for g in range(2):
            for e in range(EXPERTS):
                copies[(i * 2 + g) * EXPERTS + e].wait()
            total = jnp.dot(masked[...], buffer[i, g], preferred_element_type=jnp.float32)
            out, at = places[i]
            out[at, :, g] = total.reshape(slots, height, cols).astype(out.dtype)


def project(blocks, splits, kinds, rows, gate_weight, up_weight, slots, width):
    depth = gate_weight.shape[0]
    pairs = TOPK * rows.shape[0]
    steps = sum(splits)
    shapes = [(n, slots, 2, pairs // slots, width) for n in splits]
    weights = steps * 2 * EXPERTS * depth * width
    return pl.pallas_call(
        functools.partial(project_kernel, blocks),
        out_shape=[jax.ShapeDtypeStruct(s, k) for s, k in zip(shapes, kinds)],
        in_specs=[VMEM, ANY, ANY],
        out_specs=[VMEM] * len(splits),
        scratch_shapes=[
            pltpu.VMEM((pairs, EXPERTS * depth), jnp.bfloat16),
            pltpu.VMEM((steps, 2, EXPERTS * depth, width), jnp.bfloat16),
            pltpu.SemaphoreType.DMA((steps, 2, EXPERTS)),
        ],
        compiler_params=limit(2 * weights, 8 * steps * pairs * width),
        cost_estimate=pl.CostEstimate(
            flops=2 * pairs * weights, bytes_accessed=2 * weights, transcendentals=0
        ),
    )(rows, in_hbm(gate_weight), in_hbm(up_weight))


def mix_kernel(blocks, added, cores, routes_ref, *refs):
    steps = len(blocks)
    hidden, refs = refs[:steps], refs[steps:]
    down_ref, refs = refs[0], refs[1:]
    extra = refs[0] if added else None
    out_ref, stacked, buffer, sems = refs[-4:]
    count, depth = routes_ref.shape[0], out_ref.shape[-1]
    cols = hidden[0].shape[1]
    per_expert = down_ref.shape[1] // (EXPERTS * cols)
    copies = []
    for i, (where, d) in enumerate(blocks):
        block = where(d)
        for e in range(EXPERTS):
            first = pl.multiple_of((e * per_expert + block) * cols, cols)
            copies.append(
                pltpu.make_async_copy(
                    down_ref.at[:, pl.ds(first, cols)],
                    buffer.at[i, e],
                    sems.at[i, e],
                )
            )
            copies[-1].start()
    masks = [
        [(routes_ref[:, k : k + 1] == e).astype(jnp.float32) for k in range(TOPK)]
        for e in range(EXPERTS)
    ]
    for e in range(EXPERTS):
        keep = [jnp.broadcast_to(m, (count, cols)).astype(jnp.bfloat16) for m in masks[e]]
        for i in range(steps):
            stacked[i, e] = sum(hidden[i][k * count : (k + 1) * count] * keep[k] for k in range(TOPK))

    def step(i, total):
        for e in range(EXPERTS):
            pltpu.make_async_copy(buffer.at[i, e], buffer.at[i, e], sems.at[i, e]).wait()
        for e in range(EXPERTS):
            total += lax.dot_general(
                stacked[i, e],
                buffer[i, e],
                (((1,), (1,)), ((), ())),
                preferred_element_type=jnp.float32,
            )
        return total

    total = extra[...] if added else jnp.zeros((count, depth), jnp.float32)
    total = lax.fori_loop(0, steps, step, total).astype(out_ref.dtype)
    if not cores:
        out_ref[...] = total
    else:
        devices, own_rows, _ = out_ref.shape
        for place in range(devices):
            first = (place % cores * (devices // cores) + place // cores) * own_rows
            out_ref[place] = total[first : first + own_rows]


def mix(blocks, routes, hidden, down_weight, extra, kind, shape, cores):
    count, depth = routes.shape[0], down_weight.shape[0]
    width = hidden[0].shape[1]
    steps = len(hidden)
    room = 16 * steps * count * width
    if room > 32 * MIB and steps > 1:
        part = steps // 2
        some, whole = blocks[:part], (count, depth)
        extra = mix(some, routes, hidden[:part], down_weight, extra, jnp.float32, whole, 0)
        return mix(blocks[part:], routes, hidden[part:], down_weight, extra, kind, shape, cores)
    weights = steps * EXPERTS * depth * width
    operands = [routes, *hidden, in_hbm(down_weight)]
    specs = [VMEM] * (1 + steps) + [ANY]
    if extra is not None:
        operands.append(extra)
        specs.append(VMEM)
    return pl.pallas_call(
        functools.partial(mix_kernel, blocks, extra is not None, cores),
        out_shape=jax.ShapeDtypeStruct(shape, kind),
        in_specs=specs,
        out_specs=VMEM,
        scratch_shapes=[
            pltpu.VMEM((steps, EXPERTS, count, width), jnp.bfloat16),
            pltpu.VMEM((steps, EXPERTS, depth, width), jnp.bfloat16),
            pltpu.SemaphoreType.DMA((steps, EXPERTS)),
        ],
        compiler_params=limit(2 * weights, room),
        cost_estimate=pl.CostEstimate(
            flops=2 * count * weights, bytes_accessed=2 * weights, transcendentals=0
        ),
    )(*operands)


def shards(tokens, routes, gate_scores, gate_weight, up_weight, down_weight):
    slivers, cores = lax.axis_size("sliver"), lax.axis_size("rep")
    me, core = lax.axis_index("sliver"), lax.axis_index("rep")
    depth, columns = gate_weight.shape
    own_rows, model = tokens.shape
    devices = slivers * cores
    count = own_rows * devices
    slots = slivers // PLANE
    height = TOPK * count // slots
    width = columns // (EXPERTS * cores * PLANE * CHUNKS)

    def over_core(x):
        return lax.ppermute(x, "rep", [(i, i ^ 1) for i in range(cores)])

    def over_sliver(x, d):
        return lax.ppermute(x, "sliver", [(i, i ^ d) for i in range(slivers)])

    pieces = packed(tokens, routes, gate_scores, slivers, cores, depth)
    rows = lax.all_to_all(pieces, ("rep", "sliver"), 0, 0, tiled=True)
    rows = rows.reshape(count, depth + EXTRA)
    facts = rows[:, depth : depth + 2 * TOPK].astype(jnp.float32)
    all_routes = facts[:, :TOPK]
    all_scores = facts[:, TOPK:]
    share = all_scores / jnp.sum(all_scores, axis=1, keepdims=True)
    share = share.astype(jnp.bfloat16).astype(jnp.float32).T.reshape(slots, height, 1)
    weight = lax.dynamic_index_in_dim(share, me // PLANE, 0, keepdims=False)
    routes_padded = jnp.pad(all_routes, ((0, 0), (0, EXTRA - TOPK)))

    mine = [(own_block, d) for d in range(PLANE)]
    theirs = [(other_block, d) for d in range(PLANE)]

    def projected(blocks, splits, kinds=(jnp.float32,), before=None):
        given = rows if before is None else after(rows, before)
        return project(blocks, splits, kinds, given, gate_weight, up_weight, slots, width)

    far, far_own = projected(
        theirs[1:] + theirs[:1], (PLANE - 1, 1), (jnp.float32, jnp.bfloat16)
    )
    far, far_own = over_core(far), over_core(far_own)
    (chip,) = projected(mine[1:], (PLANE - 1,))
    chip = (chip + far).astype(jnp.bfloat16)
    (kept,) = projected(mine[:1], (1,), before=chip)
    halves = 2 if slots > 1 else 1
    top = me // (slivers // 2) if halves == 2 else 0
    length = slots // halves

    def half(x, which):
        return lax.dynamic_slice_in_dim(x, which * length, length, 0)

    terms = []
    for which in [1 - top, top][2 - halves :]:
        sent = [half(chip[d - 1], which) for d in range(1, PLANE)]
        arrived = [over_sliver(sent[d - 1], d) for d in range(1, PLANE)]
        terms.append(arrived + [half(kept[0], which), half(far_own[0], which)])

    def summed(terms):
        return sum(term.astype(jnp.float32) for term in terms)

    gathered = []
    for c in range(CHUNKS):
        distance = slivers // 2
        parts = terms[-1]
        if halves == 2:
            parts = parts + [over_sliver(summed(terms[0]).astype(jnp.bfloat16), distance)]
            distance //= 2
        while distance >= PLANE:
            bit = (me // distance) % 2
            length = parts[0].shape[0] // 2

            def part(which):
                return summed(
                    [lax.dynamic_slice_in_dim(x, which * length, length, 0) for x in parts]
                )

            other = over_sliver(part(1 - bit).astype(jnp.bfloat16), distance)
            parts = [part(bit), other]
            distance //= 2
        total = sum(term.astype(jnp.float32) for term in parts)[0]
        hidden = (jax.nn.silu(total[0]) * total[1] * weight).astype(jnp.bfloat16)[None]
        distance = PLANE
        while distance < slivers:
            bit = (me // distance) % 2
            other = over_sliver(hidden, distance)
            hidden = jnp.where(
                bit == 0,
                jnp.concatenate([hidden, other], axis=0),
                jnp.concatenate([other, hidden], axis=0),
            )
            distance *= 2
        hidden = hidden.reshape(TOPK * count, width)
        gathered.append([hidden] + [over_sliver(hidden, d) for d in range(1, PLANE)])

    (gathered,) = gathered
    order = mine[:1] + theirs[:1]
    first = [gathered[0], over_core(gathered[0])]
    shape = (count, depth)
    mixed = mix(order, routes_padded, first, down_weight, None, jnp.float32, shape, 0)
    last = PLANE - 1
    early = after(gathered[last], mixed)
    early_other = over_core(early)
    mixed = mix(mine[last:], routes_padded, [early], down_weight, mixed, jnp.float32, shape, 0)
    rest = [after(x, mixed) for x in gathered[1:last]]
    rest += [over_core(x) for x in rest] + [early_other]
    order = mine[1:last] + theirs[1:]
    shape = (devices, own_rows, depth)
    pieces = mix(order, routes_padded, rest, down_weight, mixed, jnp.bfloat16, shape, cores)
    pieces = lax.all_to_all(pieces, ("sliver", "rep"), 0, 0, tiled=True)
    return jnp.transpose(pieces, (1, 0, 2)).reshape(own_rows, model)


def solution(mesh):
    return jax.shard_map(
        shards,
        mesh=mesh,
        in_specs=(
            P(("group", "rep", "sliver"), None),
            P(("group", "rep", "sliver"), None),
            P(("group", "rep", "sliver"), None),
            P(("group", "sliver", "rep"), None),
            P(("group", "sliver", "rep"), None),
            P(("group", "sliver", "rep"), None),
        ),
        out_specs=P(("group", "rep", "sliver"), None),
        check_vma=False,
    )
```
